32 devices in a mesh: grp: 2 (over y), view: 4 (over z), slab: 2 (over x), rep: 2 (over core).
Axes of the slice: x: 2, y: 2, z: 4, core: 2. Of those that a mesh axis runs over, the one named last changes fastest.
Arguments:
- images: float32 [3, 4, 512, 512], P(None, ('grp', 'slab'), ('view', 'rep')), parts along dimension 1, may hold values from -6 to 6
- scaled_duals: float32 [9, 4, 512, 512], P(None, ('grp', 'slab'), ('view', 'rep')), parts along dimension 1, may hold values from -3 to 3
- proj_tiles: bfloat16 [48, 128, 128], replicated, may hold values from -0.5 to 0.5
- tile_ids: int32 [4, 256], replicated, may hold values from 0 to 47
- pixel_blocks: int32 [4, 256], replicated, may hold values from 0 to 2047
- tof_offsets: int32 [4, 256], replicated, may hold values from 0 to 1920
- counts: int32 [4], replicated, may hold values from 32 to 256, as said below
- sinogram: bfloat16 [4, 8192], P(('grp', 'slab')), parts along dimension 0, may hold values from -12 to 12
- coil_maps: float32 [2, 4, 4, 4, 2, 64, 512], P(None, 'view', ('grp', 'slab'), None, 'rep'), parts along dimension 2, may hold values from -2.1213202 to 2.1213202
- kspace: float32 [2, 4, 4, 4, 2, 64, 512], P(None, 'view', ('grp', 'slab'), None, 'rep'), parts along dimension 2, may hold values from -0.9 to 0.9
- sampling: int32 [4, 4, 2, 64], P(('grp', 'slab'), None, 'rep'), parts along dimension 0, may hold values 0 or 1
Outputs:
- updated: float32 [3, 4, 512, 512], P(None, ('grp', 'slab'), ('view', 'rep')), parts along dimension 1
- shrunk: float32 [9, 4, 512, 512], P(None, ('grp', 'slab'), ('view', 'rep')), parts along dimension 1
- dual_next: float32 [9, 4, 512, 512], P(None, ('grp', 'slab'), ('view', 'rep')), parts along dimension 1
The draws below stay inside these ranges and needn't reach their ends.
There are 2 independent parts, one for each index of `grp`. The reference program is written for one: setup_inputs(seed, part) draws one part's arguments, and reference() takes and returns one part's arrays. A program takes and returns all parts, laid end to end along the dimension named above; an argument that names none is the same for every part. Nothing has to cross between parts.
Inputs may be any that keep to these rules, and one draw needn't show every extreme that they name: Slots j < counts[v] of sector v are live and the others unused; some sector has all 256 slots live.
All inputs are finite; a program needn't handle non-finite values. No bound on the sum of `sampling` on one device may be relied on, other than what follows from the above.
Results may differ from the reference program's by a relative error of at most 0.0024.
Values sent between devices are 32-bit elements; how exact they have to be, the bound alone decides.
A program may use at most 64 MiB of HBM per device.

```python
import jax
import jax.numpy as jnp
from jax import lax

N = 512
TILE = 128
SBINS = 2048
NTILE = 48
CAP = 256
SECTORS = 4
COILS = 4
SLICES = 2
ROWB = 64
PBLK = 2048
N_VIEW = 4
N_REP = 2


def draw_counts(key, part):
    key = jax.random.fold_in(key, 7)
    random_pick = jax.random.randint(key, (SECTORS,), 0, CAP)
    shaped = jnp.maximum(CAP // 8, random_pick * random_pick // CAP)
    fullest = jax.random.randint(jax.random.fold_in(key, 1), (), 0, SECTORS)
    return jnp.where(jnp.arange(SECTORS) == fullest, CAP, shaped).astype(jnp.int32)


def set_ends(values, key, least, top_value):
    longest = values.shape.index(max(values.shape))
    spots = []
    for shift in (0, 1):
        where = [jax.random.randint(jax.random.fold_in(key, axis), (), 0, length) for axis, length in enumerate(values.shape)]
        where[longest] = (where[longest] + shift) % values.shape[longest]
        spots.append(tuple(where))
    return values.at[spots[0]].set(least).at[spots[1]].set(top_value)


def block_scale(key, dims, shards, low, largest):
    factor_of = 1.0
    for dim, parts in shards:
        draws = jax.random.uniform(jax.random.fold_in(jax.random.fold_in(key, 6), dim), (parts,), jnp.float32, low / len(shards), largest / len(shards))
        factor_of = factor_of * jnp.repeat(jnp.exp(draws), dims[dim] // parts).reshape((-1,) + (1,) * (len(dims) - 1 - dim))
    return factor_of


def normal_values(own_key, extent, deviation, bound, pieces=(), kind=jnp.bfloat16):
    values = deviation * jax.random.normal(own_key, extent, jnp.float32)
    if pieces:
        values = values * block_scale(own_key, extent, pieces, -0.22, 0.18)
    return jnp.clip(values, -bound, bound).astype(kind)


def setup_inputs(seed: int = 0, part: int = 0) -> dict:
    keys = jax.random.split(jax.random.key(seed), 12)
    part_splits = jax.random.split(jax.random.fold_in(keys[11], part), 12)
    images = normal_values(part_splits[0], (3, SLICES, N, N), 1.0, 6.0, ((1, 2), (2, 8)), jnp.float32)
    scaled_duals = normal_values(part_splits[1], (9, SLICES, N, N), 0.5, 3.0, ((1, 2), (2, 8)), jnp.float32)
    proj_tiles = normal_values(keys[2], (NTILE, TILE, TILE), TILE ** -0.5, 0.5)
    tile_ids = set_ends(jax.random.randint(keys[3], (SECTORS, CAP), 0, NTILE), jax.random.fold_in(keys[3], 1), 0, NTILE - 1).astype(jnp.int32)
    pixel_blocks = set_ends(jax.random.randint(keys[4], (SECTORS, CAP), 0, PBLK), jax.random.fold_in(keys[4], 1), 0, PBLK - 1).astype(jnp.int32)
    tof_offsets = set_ends(jax.random.randint(keys[5], (SECTORS, CAP), 0, SBINS - TILE + 1), jax.random.fold_in(keys[5], 1), 0, SBINS - TILE).astype(jnp.int32)
    counts = draw_counts(jax.random.fold_in(keys[11], 71), part)
    sinogram = normal_values(part_splits[7], (SLICES, SECTORS * SBINS), 2.0, 12.0, ((0, 2),))
    coil_maps = normal_values(part_splits[8], (2, COILS, SLICES, N_VIEW, N_REP, ROWB, N), ((2 * COILS) ** -0.5), 2.1213202, ((1, 4), (2, 2), (4, 2)), jnp.float32)
    kspace = normal_values(part_splits[9], (2, COILS, SLICES, N_VIEW, N_REP, ROWB, N), 0.15, 0.9, ((1, 4), (2, 2), (4, 2)), jnp.float32)
    sampling = set_ends((jax.random.randint(part_splits[10], (SLICES, N_VIEW, N_REP, ROWB), 0, 2) < 1).astype(jnp.int32), jax.random.fold_in(part_splits[10], 1), 0, 1)
    return dict(images=images, scaled_duals=scaled_duals, proj_tiles=proj_tiles, tile_ids=tile_ids, pixel_blocks=pixel_blocks, tof_offsets=tof_offsets, counts=counts, sinogram=sinogram, coil_maps=coil_maps, kspace=kspace, sampling=sampling)


kappa = 4.0
step_size = 0.4
penalty = 0.5

def forward_diff(values, axis):
    length = values.shape[axis]
    shifted = jnp.concatenate([lax.slice_in_dim(values, 1, length, axis=axis), jnp.zeros_like(lax.slice_in_dim(values, 0, 1, axis=axis))], axis=axis)
    shape = [1] * values.ndim
    shape[axis] = length
    keeper = (jnp.arange(length) < length - 1).reshape(shape).astype(values.dtype)
    return (shifted - values) * keeper

def adjoint_diff(values, axis):
    length = values.shape[axis]
    shape = [1] * values.ndim
    shape[axis] = length
    keeper = (jnp.arange(length) < length - 1).reshape(shape).astype(values.dtype)
    masked = values * keeper
    earlier = jnp.concatenate([jnp.zeros_like(lax.slice_in_dim(masked, 0, 1, axis=axis)), lax.slice_in_dim(masked, 0, length - 1, axis=axis)], axis=axis)
    return earlier - masked

def reference(images, scaled_duals, proj_tiles, tile_ids, pixel_blocks, tof_offsets, counts, sinogram, coil_maps, kspace, sampling):
    slices = images.shape[1]
    pet_low = images[0].astype(jnp.bfloat16).reshape(slices, PBLK, TILE)
    lane_index = jnp.arange(TILE, dtype=jnp.int32)
    slot_index = jnp.arange(CAP, dtype=jnp.int32)

    def sector_forward(carry, packed_stack):
        sector_ids, sector_blocks, sector_offsets, sector_count = packed_stack
        tile_mats = proj_tiles[sector_ids].astype(jnp.float32)
        pixels = pet_low[:, sector_blocks, :].astype(jnp.float32)
        contrib = jnp.einsum('jbt,sjt->sjb', tile_mats, pixels)
        live_flag = (slot_index < sector_count).astype(jnp.float32)
        contrib = contrib * live_flag[None, :, None]
        positions = sector_offsets[:, None] + lane_index[None, :]
        sector_sino = jnp.zeros((slices, SBINS), jnp.float32).at[:, positions].add(contrib)
        return (carry, sector_sino)
    unused, projected = lax.scan(sector_forward, jnp.zeros((), jnp.float32), (tile_ids, pixel_blocks, tof_offsets, counts))
    measured = jnp.transpose(sinogram.reshape(slices, SECTORS, SBINS), (1, 0, 2))
    pet_residual = (projected - measured).astype(jnp.bfloat16)

    def sector_back(partial_value, packed_stack):
        sector_ids, sector_blocks, sector_offsets, sector_count, sector_resid = packed_stack
        tile_mats = proj_tiles[sector_ids].astype(jnp.float32)
        positions = sector_offsets[:, None] + lane_index[None, :]
        segments = sector_resid[:, positions].astype(jnp.float32)
        live_flag = (slot_index < sector_count).astype(jnp.float32)
        back = jnp.einsum('jbt,sjb->sjt', tile_mats, segments) * live_flag[None, :, None]
        return (partial_value.at[:, sector_blocks, :].add(back), jnp.zeros((), jnp.float32))
    back_projected, unused_two = lax.scan(sector_back, jnp.zeros((slices, PBLK, TILE), jnp.float32), (tile_ids, pixel_blocks, tof_offsets, counts, pet_residual))
    back_projected = back_projected.reshape(1, slices, N, N)
    sens = coil_maps.reshape(2, COILS, slices, N, N)
    measured_k = kspace.reshape(2, COILS, slices, N, N)
    acquired_samples = sampling.reshape(slices, N).astype(jnp.float32)[:, :, None]
    image_mr = lax.complex(images[1], images[2])

    def one_coil(summed, packed_stack):
        sensitivity_real, sensitivity_imaginary, measured_real, measured_imaginary = packed_stack
        smap = lax.complex(sensitivity_real, sensitivity_imaginary)
        fourier_spectrum = jnp.fft.fft2(smap * image_mr, norm='ortho')
        kspace_residual = acquired_samples * (fourier_spectrum - lax.complex(measured_real, measured_imaginary))
        back = jnp.conj(smap) * jnp.fft.ifft2(kspace_residual, norm='ortho')
        return (summed + jnp.stack([jnp.real(back), jnp.imag(back)]), jnp.zeros((), jnp.float32))
    coil_gradient, unused_three = lax.scan(one_coil, jnp.zeros((2, slices, N, N), jnp.float32), (sens[0], sens[1], measured_k[0], measured_k[1]))
    data_gradient = jnp.concatenate([back_projected, coil_gradient], axis=0)
    axes_order = (1, 2, 0)
    differences = jnp.stack([jnp.stack([forward_diff(images[channel], axis) for axis in axes_order]) for channel in range(3)]).reshape(9, slices, N, N)
    spread = differences + scaled_duals
    magnitude = jnp.sqrt(lax.optimization_barrier(jnp.sum(spread * spread, axis=0)))
    shrunk = spread * (jnp.maximum(magnitude - kappa, 0.0) / jnp.maximum(magnitude, kappa))[None]
    dual_next = spread - shrunk
    coupling = differences - shrunk + dual_next
    adjoint = jnp.stack([sum((adjoint_diff(coupling[channel * 3 + which], axes_order[which]) for which in range(3))) for channel in range(3)])
    updated = images - step_size * (data_gradient + penalty * adjoint)
    return (updated, shrunk, dual_next)
```

```python
import math

import jax
import jax.numpy as jnp
import ml_dtypes
import numpy as np
from jax import lax
from jax.experimental import pallas as pl
from jax.experimental.pallas import tpu as pltpu
from jax.sharding import PartitionSpec as P

kappa = 4.0
step_size = 0.4
penalty = 0.5
bf16 = jnp.bfloat16
f32 = jnp.float32


def contract(left, right, left_dim, right_dim):
    return lax.dot_general(
        left, right, (((left_dim,), (right_dim,)), ((), ())), preferred_element_type=f32
    )


def split_table(table):
    high = table.astype(ml_dtypes.bfloat16)
    low = (table - high.astype(np.float64)).astype(ml_dtypes.bfloat16)
    return high, low


def split_data(values):
    high = values.astype(bf16)
    return high, (values - high.astype(f32)).astype(bf16)


def one_hot(count, index):
    rows = lax.broadcasted_iota(jnp.int32, (count, index.shape[1]), 0)
    return jnp.where(rows == index, 1.0, 0.0).astype(bf16)


def masked_pair(values, ids, pair):
    parts = []
    for which in range(2):
        flag = jnp.where(ids == 2 * pair + which, 1.0, 0.0).astype(bf16)
        parts.append(values * flag)
    return jnp.concatenate(parts, axis=0)


def project_kernel(info_ref, rows_ref, tiles_ref, sino_ref, total):
    local, ids, start = info_ref[0, 0:1], info_ref[0, 1:2], info_ref[0, 2:3]
    tile = tiles_ref.shape[1]
    pixels = contract(rows_ref[...], one_hot(rows_ref.shape[0], local), 0, 0).astype(bf16)
    total[...] = jnp.zeros_like(total)

    def step(pair, carry):
        tiles = jnp.concatenate([tiles_ref[2 * pair], tiles_ref[2 * pair + 1]], axis=1)
        total[...] += contract(tiles, masked_pair(pixels, ids, pair), 1, 0)
        return carry

    lax.fori_loop(0, tiles_ref.shape[0] // 2, step, 0)
    moved = jnp.concatenate([total[...], jnp.zeros_like(total)], axis=0)
    shift = start % tile
    for bit in range(int(math.log2(tile))):
        moved = jnp.where((shift >> bit) & 1 == 1, pltpu.roll(moved, 1 << bit, 0), moved)
    bins = start // tile
    rows = sino_ref.shape[0]

    @pl.when(pl.program_id(0) == 0)
    def _():
        sino_ref[...] = jnp.zeros_like(sino_ref)

    for half in range(2):
        place = one_hot(rows, bins + half)
        rest = moved[half * tile : (half + 1) * tile]
        for _ in range(3):
            part = rest.astype(bf16)
            sino_ref[...] += contract(place, part, 1, 1)
            rest = rest - part.astype(f32)


def back_kernel(info_ref, resid_ref, tiles_ref, back_ref, total):
    local, ids, start = info_ref[0, 0:1], info_ref[0, 1:2], info_ref[0, 2:3]
    tile = tiles_ref.shape[1]
    bins = start // tile
    shift = start % tile
    resid = resid_ref[...]
    moved = jnp.concatenate(
        [contract(resid, one_hot(resid.shape[0], bins + half), 0, 0) for half in range(2)], axis=0
    )
    for bit in range(int(math.log2(tile))):
        moved = jnp.where(
            (shift >> bit) & 1 == 1, pltpu.roll(moved, 2 * tile - (1 << bit), 0), moved
        )
    window = moved[:tile].astype(bf16)
    total[...] = jnp.zeros_like(total)

    def step(pair, carry):
        tiles = jnp.concatenate([tiles_ref[2 * pair], tiles_ref[2 * pair + 1]], axis=0)
        total[...] += contract(tiles, masked_pair(window, ids, pair), 0, 0)
        return carry

    lax.fori_loop(0, tiles_ref.shape[0] // 2, step, 0)

    @pl.when(pl.program_id(0) == 0)
    def _():
        back_ref[...] = jnp.zeros_like(back_ref)

    place = one_hot(back_ref.shape[0], local)
    rest = total[...]
    for _ in range(3):
        part = rest.astype(bf16)
        back_ref[...] += contract(place, part, 1, 1)
        rest = rest - part.astype(f32)


def tile_call(kernel, info, values, tiles, rows):
    chunks, _, chunk = info.shape
    tile = tiles.shape[1]
    return pl.pallas_call(
        kernel,
        grid=(chunks,),
        out_shape=jax.ShapeDtypeStruct((rows, tile), f32),
        in_specs=[
            pl.BlockSpec((1, 8, chunk), lambda i: (i, 0, 0)),
            pl.BlockSpec(values.shape, lambda i: (0, 0)),
            pl.BlockSpec(tiles.shape, lambda i: (0, 0, 0)),
        ],
        out_specs=pl.BlockSpec((rows, tile), lambda i: (0, 0)),
        scratch_shapes=[pltpu.VMEM((tile, chunk), f32)],
        compiler_params=pltpu.CompilerParams(vmem_limit_bytes=32 * 1024 * 1024),
        cost_estimate=pl.CostEstimate(
            flops=2 * chunks * chunk * tiles.size, bytes_accessed=2 * tiles.size, transcendentals=0
        ),
    )(info, values, tiles)


def on_device(
    images,
    scaled_duals,
    proj_tiles,
    tile_ids,
    pixel_blocks,
    tof_offsets,
    counts,
    sinogram,
    coil_maps,
    kspace,
    sampling,
):
    rep_count = lax.axis_size("rep")
    owner_count = lax.axis_size("view") * rep_count
    slab_count = lax.axis_size("slab")
    rep_at = lax.axis_index("rep")
    slab_at = lax.axis_index("slab")
    owner_at = lax.axis_index("view") * rep_count + rep_at
    row_block = images.shape[2]
    width = images.shape[3]
    tile_size = proj_tiles.shape[1]
    sectors, capacity = tile_ids.shape
    sector_bins = sinogram.shape[1] // sectors
    groups = coil_maps.shape[3]

    own_images = images[:, 0]
    ring = [(i, i + 1) for i in range(owner_count - 1)]
    row_after = lax.ppermute(own_images[:, :1], ("view", "rep"), [(b, a) for a, b in ring])
    chain = [(i, i + 1) for i in range(slab_count - 1)]
    slice_after = lax.ppermute(own_images, "slab", [(b, a) for a, b in chain])

    gathered = lax.all_gather(images[1:3, 0], "view", axis=1, tiled=True)
    own_image = gathered.reshape(2, groups * row_block, width)

    own_blocks = row_block * width // tile_size
    local = pixel_blocks - owner_at * own_blocks
    live = jnp.arange(capacity, dtype=jnp.int32)[None] < counts[:, None]
    local = jnp.where(live & (local >= 0) & (local < own_blocks), local, -1)
    start = tof_offsets + sector_bins * jnp.arange(sectors, dtype=jnp.int32)[:, None]
    chunk = 4 * capacity
    lists = [part.reshape(-1, 1, chunk) for part in (local, tile_ids, start)]
    info = jnp.concatenate(lists + [jnp.zeros_like(lists[0])] * 5, axis=1)
    pixel_rows = own_images[0].astype(bf16).reshape(-1, tile_size)
    bin_rows = sinogram.shape[1] // tile_size
    projected = tile_call(project_kernel, info, pixel_rows, proj_tiles, bin_rows)
    full_sino = lax.psum(projected, ("view", "rep"))
    measured = sinogram[0].reshape(bin_rows, tile_size).astype(f32)
    pet_residual = (full_sino - measured).astype(bf16)
    pet_term = tile_call(back_kernel, info, pet_residual, proj_tiles, own_blocks)
    pet_term = pet_term.reshape(row_block, width)

    grid = np.arange(width)
    angle = (np.outer(grid, grid) % width) * (2.0 * np.pi / width)
    cosine, sine = np.cos(angle) / np.sqrt(width), np.sin(angle) / np.sqrt(width)
    by_rep = grid.reshape(groups, rep_count, row_block).transpose(1, 0, 2).reshape(rep_count, -1)
    rep_major = by_rep.reshape(-1)
    row_tables = np.stack(
        [
            np.concatenate([table[rows][:, rep_major] for table in (cosine, sine)], axis=0)
            for rows in by_rep
        ]
    )
    row_high, row_low = (
        lax.dynamic_index_in_dim(jnp.asarray(part), rep_at, keepdims=False)
        for part in split_table(row_tables)
    )
    forward = np.block([[cosine, -sine], [sine, cosine]])
    inverse = np.block([[cosine, sine], [-sine, cosine]])

    def columns(real, imag, table):
        high, low = split_data(jnp.concatenate([real, imag], axis=1))
        table_high, table_low = (jnp.asarray(part) for part in split_table(table))
        return (
            contract(high, table_high, 1, 0)
            + contract(low, table_high, 1, 0)
            + contract(high, table_low, 1, 0)
        )

    def rows(values):
        both = lax.all_gather(values, "rep", axis=0, tiled=True)
        high, low = split_data(both)
        out = (
            contract(row_high, high, 1, 0)
            + contract(row_high, low, 1, 0)
            + contract(row_low, high, 1, 0)
        )
        half = out.shape[0] // 2
        return (
            out[:half, :width],
            out[:half, width:],
            out[half:, :width],
            out[half:, width:],
        )

    sens = coil_maps.reshape(2, groups * row_block, width)
    coil_re = sens[0] * own_image[0] - sens[1] * own_image[1]
    coil_im = sens[0] * own_image[1] + sens[1] * own_image[0]
    cos_re, cos_im, sin_re, sin_im = rows(columns(coil_re, coil_im, forward))
    measured_k = kspace.reshape(2, groups * row_block, width)
    acquired = sampling.reshape(-1).astype(f32)[:, None]
    resid_re = acquired * (cos_re + sin_im - measured_k[0])
    resid_im = acquired * (cos_im - sin_re - measured_k[1])
    cos_re, cos_im, sin_re, sin_im = rows(columns(resid_re, resid_im, inverse))
    image_re = cos_re - sin_im
    image_im = cos_im + sin_re
    grad_re = sens[0] * image_re + sens[1] * image_im
    grad_im = sens[0] * image_im - sens[1] * image_re
    coil_rows = jnp.stack([grad_re, grad_im]).reshape(2, groups, row_block, width)
    coil_gradient = lax.psum_scatter(coil_rows, "view", scatter_dimension=1, tiled=True)
    data_gradient = jnp.concatenate([pet_term[None], coil_gradient[:, 0]], axis=0)

    global_rows = owner_at * row_block + jnp.arange(row_block, dtype=jnp.int32)
    row_keep = (global_rows < width - 1).astype(f32)[None, :, None]
    slice_keep = (slab_at < slab_count - 1).astype(f32)
    column_keep = (jnp.arange(width) < width - 1).astype(f32)[None, None, :]
    next_row = jnp.concatenate([own_images[:, 1:], row_after], axis=1)
    next_column = jnp.concatenate([own_images[..., 1:], own_images[..., :1]], axis=-1)
    diff_rows = (next_row - own_images) * row_keep
    diff_columns = (next_column - own_images) * column_keep
    diff_slices = (slice_after - own_images) * slice_keep
    differences = jnp.stack([diff_rows, diff_columns, diff_slices], axis=1).reshape(
        9, row_block, width
    )
    spread = differences + scaled_duals[:, 0]
    magnitude = jnp.sqrt(jnp.sum(spread * spread, axis=0))
    shrunk = spread * (jnp.maximum(magnitude - kappa, 0.0) / jnp.maximum(magnitude, kappa))[None]
    dual_next = spread - shrunk
    coupling = (differences - shrunk + dual_next).reshape(3, 3, row_block, width)
    couple_rows = coupling[:, 0] * row_keep
    couple_columns = coupling[:, 1] * column_keep
    couple_slices = coupling[:, 2] * slice_keep
    row_before = lax.ppermute(couple_rows[:, -1:], ("view", "rep"), ring)
    slice_before = lax.ppermute(couple_slices, "slab", chain)
    adjoint = (
        jnp.concatenate([row_before, couple_rows[:, :-1]], axis=1)
        - couple_rows
        + jnp.concatenate([couple_columns[..., -1:], couple_columns[..., :-1]], axis=-1)
        - couple_columns
        + slice_before
        - couple_slices
    )
    updated = own_images - step_size * (data_gradient + penalty * adjoint)
    return (updated[:, None], shrunk[:, None], dual_next[:, None])


def solution(mesh):
    placed = (
        P(None, ("grp", "slab"), ("view", "rep"), None),
        P(None, ("grp", "slab"), ("view", "rep"), None),
        P(),
        P(),
        P(),
        P(),
        P(),
        P(("grp", "slab"), None),
        P(None, "view", ("grp", "slab"), None, "rep", None, None),
        P(None, "view", ("grp", "slab"), None, "rep", None, None),
        P(("grp", "slab"), None, "rep", None),
    )
    return jax.shard_map(
        on_device,
        mesh=mesh,
        in_specs=placed,
        out_specs=(
            P(None, ("grp", "slab"), ("view", "rep"), None),
            P(None, ("grp", "slab"), ("view", "rep"), None),
            P(None, ("grp", "slab"), ("view", "rep"), None),
        ),
        check_vma=False,
    )
```

```python
import functools
import math

import jax
import jax.numpy as jnp
import ml_dtypes
import numpy as np
from jax import lax
from jax.experimental import pallas as pl
from jax.experimental.pallas import tpu as pltpu
from jax.sharding import PartitionSpec as P

kappa = 4.0
step_size = 0.4
penalty = 0.5
bf16 = jnp.bfloat16
f32 = jnp.float32


def contract(left, right, left_dim, right_dim):
    return lax.dot_general(
        left, right, (((left_dim,), (right_dim,)), ((), ())), preferred_element_type=f32
    )


def split_table(table):
    high = table.astype(ml_dtypes.bfloat16)
    low = (table - high.astype(np.float64)).astype(ml_dtypes.bfloat16)
    return high, low


def split_data(values):
    high = values.astype(bf16)
    return high, (values - high.astype(f32)).astype(bf16)


def one_hot(count, index):
    rows = lax.broadcasted_iota(jnp.int32, (count, index.shape[1]), 0)
    return jnp.where(rows == index, 1.0, 0.0).astype(bf16)


def masked_pair(values, ids, pair):
    parts = []
    for which in range(2):
        flag = jnp.where(ids == 2 * pair + which, 1.0, 0.0).astype(bf16)
        parts.append(values * flag)
    return jnp.concatenate(parts, axis=0)


def project(info_ref, at, rows_ref, tiles_ref, sino_ref, total):
    local, ids, start = info_ref[at, 0:1], info_ref[at, 1:2], info_ref[at, 2:3]
    tile = tiles_ref.shape[1]
    pixels = contract(rows_ref[...], one_hot(rows_ref.shape[0], local), 0, 0).astype(bf16)
    total[...] = jnp.zeros_like(total)

    def step(pair, carry):
        tiles = jnp.concatenate([tiles_ref[2 * pair], tiles_ref[2 * pair + 1]], axis=1)
        total[...] += contract(tiles, masked_pair(pixels, ids, pair), 1, 0)
        return carry

    lax.fori_loop(0, tiles_ref.shape[0] // 2, step, 0)
    moved = jnp.concatenate([total[...], jnp.zeros_like(total)], axis=0)
    shift = start % tile
    for bit in range(int(math.log2(tile))):
        moved = jnp.where((shift >> bit) & 1 == 1, pltpu.roll(moved, 1 << bit, 0), moved)
    bins = start // tile
    rows = sino_ref.shape[0]
    for half in range(2):
        place = one_hot(rows, bins + half)
        rest = moved[half * tile : (half + 1) * tile]
        for _ in range(3):
            part = rest.astype(bf16)
            sino_ref[...] += contract(place, part, 1, 1)
            rest = rest - part.astype(f32)


def back_project(info_ref, at, resid, tiles_ref, back_ref, total):
    local, ids, start = info_ref[at, 0:1], info_ref[at, 1:2], info_ref[at, 2:3]
    tile = tiles_ref.shape[1]
    bins = start // tile
    shift = start % tile
    moved = jnp.concatenate(
        [contract(resid, one_hot(resid.shape[0], bins + half), 0, 0) for half in range(2)], axis=0
    )
    for bit in range(int(math.log2(tile))):
        moved = jnp.where(
            (shift >> bit) & 1 == 1, pltpu.roll(moved, 2 * tile - (1 << bit), 0), moved
        )
    window = moved[:tile].astype(bf16)
    total[...] = jnp.zeros_like(total)

    def step(pair, carry):
        tiles = jnp.concatenate([tiles_ref[2 * pair], tiles_ref[2 * pair + 1]], axis=0)
        total[...] += contract(tiles, masked_pair(window, ids, pair), 0, 0)
        return carry

    lax.fori_loop(0, tiles_ref.shape[0] // 2, step, 0)
    place = one_hot(back_ref.shape[0], local)
    rest = total[...]
    for _ in range(3):
        part = rest.astype(bf16)
        back_ref[...] += contract(place, part, 1, 1)
        rest = rest - part.astype(f32)


MESH = pl.DeviceIdType.MESH


def remote(source, target, send_sem, recv_sem, device):
    return pltpu.make_async_remote_copy(
        src_ref=source,
        dst_ref=target,
        send_sem=send_sem,
        recv_sem=recv_sem,
        device_id=device,
        device_id_type=MESH,
    )


def greet(devices):
    barrier = pltpu.get_barrier_semaphore()
    for device in devices:
        pl.semaphore_signal(barrier, inc=1, device_id=device, device_id_type=MESH)
    pl.semaphore_wait(barrier, len(devices))


def gather_kernel(
    views,
    reps,
    info_ref,
    rows_ref,
    tiles_ref,
    measured_ref,
    own_ref,
    gathered_ref,
    back_ref,
    total,
    sino,
    slots,
    send_rows,
    recv_rows,
    send_sino,
    recv_sino,
):
    view, rep = lax.axis_index("view"), lax.axis_index("rep")
    count = views * reps
    me = view * reps + rep

    def owner(index):
        index = lax.rem(index, count)
        return {"view": index // reps, "rep": lax.rem(index, reps)}

    greet([owner(me + step) for step in range(1, count)])
    copies = []
    for step in range(1, views):
        device = {"view": lax.rem(view + step, views), "rep": rep}
        copy = remote(
            own_ref, gathered_ref.at[view], send_rows.at[step], recv_rows.at[step], device
        )
        copy.start()
        copies.append(copy)
    gathered_ref[view] = own_ref[...]
    sino[...] = jnp.zeros_like(sino)
    for at in range(info_ref.shape[0]):
        project(info_ref, at, rows_ref, tiles_ref, sino, total)
    sums = []
    for step in range(1, count):
        copy = remote(
            sino, slots.at[step], send_sino.at[step], recv_sino.at[step], owner(me + step)
        )
        copy.start()
        sums.append(copy)
    for copy in sums:
        copy.wait()
    full = sino[...]
    for step in range(1, count):
        full = full + slots[step]
    resid = (full - measured_ref[...].astype(f32)).astype(bf16)
    back_ref[...] = jnp.zeros_like(back_ref)
    for at in range(info_ref.shape[0]):
        back_project(info_ref, at, resid, tiles_ref, back_ref, total)
    for step in range(1, views):
        source = lax.rem(view + views - step, views)
        remote(
            own_ref,
            gathered_ref.at[source],
            send_rows.at[step],
            recv_rows.at[step],
            {"view": source, "rep": rep},
        ).wait_recv()
    for copy in copies:
        copy.wait_send()


def gather_call(views, reps, info, rows, tiles, measured, own):
    chunk = info.shape[2]
    tile = tiles.shape[1]
    vmem = pl.BlockSpec(memory_space=pltpu.VMEM)
    dma = pltpu.SemaphoreType.DMA
    return pl.pallas_call(
        functools.partial(gather_kernel, views, reps),
        out_shape=(
            jax.ShapeDtypeStruct((views, *own.shape), f32),
            jax.ShapeDtypeStruct(rows.shape, f32),
        ),
        in_specs=[vmem] * 5,
        out_specs=(vmem, vmem),
        scratch_shapes=[
            pltpu.VMEM((tile, chunk), f32),
            pltpu.VMEM(measured.shape, f32),
            pltpu.VMEM((views * reps, *measured.shape), f32),
            dma((views,)),
            dma((views,)),
            dma((views * reps,)),
            dma((views * reps,)),
        ],
        compiler_params=pltpu.CompilerParams(
            collective_id=0, has_side_effects=True, vmem_limit_bytes=48 * 1024 * 1024
        ),
        cost_estimate=pl.CostEstimate(
            flops=4 * info.shape[0] * chunk * tiles.size,
            bytes_accessed=8 * own.size * views,
            transcendentals=0,
        ),
    )(info, rows, tiles, measured, own)


def split_product(left, right):
    return (
        contract(left[0], right[0], 1, 0)
        + contract(left[1], right[0], 1, 0)
        + contract(left[0], right[1], 1, 0)
    )


def coil_kernel(
    views,
    reps,
    gathered_ref,
    maps_ref,
    kspace_ref,
    acquired_ref,
    column_high,
    column_low,
    row_high,
    row_low,
    out_ref,
    buffers,
    total,
    resid,
    grads,
    arrived,
    send_rep,
    recv_rep,
    send_view,
    recv_view,
):
    view, rep = lax.axis_index("view"), lax.axis_index("rep")
    rows, width = maps_ref.shape[1], maps_ref.shape[2]
    row_block = gathered_ref.shape[2]
    halves = 2
    part = rows // halves
    near = [{"view": view, "rep": lax.rem(rep + step, reps)} for step in range(1, reps)]
    far = [{"view": lax.rem(view + step, views), "rep": rep} for step in range(1, views)]
    greet(near + far)
    sends = []

    def columns(stage, half, real, imag, sign):
        table = (column_high[...], column_low[...])
        out = split_product(split_data(jnp.concatenate([real, imag], axis=0)), table)
        where = pl.ds(half * part, part)
        buffers[stage, 0, where, :width] = out[:part, :width] + sign * out[part:, width:]
        buffers[stage, 0, where, width:] = out[part:, :width] - sign * out[:part, width:]
        for step in range(1, reps):
            index = (stage * halves + half) * reps + step
            copy = remote(
                buffers.at[stage, 0, where],
                buffers.at[stage, step, where],
                send_rep.at[index],
                recv_rep.at[index],
                near[step - 1],
            )
            copy.start()
            sends.append(copy)

    def row_products(stage):
        for step in range(reps):
            if step:
                for half in range(halves):
                    sends[(stage * halves + half) * (reps - 1) + step - 1].wait_recv()
            where = pl.ds(step * rows, rows)
            table = (row_high[:, where], row_low[:, where])
            product = split_product(table, split_data(buffers[stage, step]))
            if step:
                total[...] += product
            else:
                total[...] = product

    blocks = part // row_block
    for half in range(halves):
        where = pl.ds(half * part, part)
        real = gathered_ref[half * blocks : (half + 1) * blocks, 0].reshape(part, width)
        imag = gathered_ref[half * blocks : (half + 1) * blocks, 1].reshape(part, width)
        map_re, map_im = maps_ref[0, where], maps_ref[1, where]
        columns(0, half, map_re * real - map_im * imag, map_re * imag + map_im * real, 1.0)
    row_products(0)
    acquired = acquired_ref[...]
    resid[0] = acquired * (total[:rows, :width] + total[rows:, width:] - kspace_ref[0])
    resid[1] = acquired * (total[:rows, width:] - total[rows:, :width] - kspace_ref[1])
    for half in range(halves):
        where = pl.ds(half * part, part)
        columns(1, half, resid[0, where], resid[1, where], -1.0)
    row_products(1)
    image_re = total[:rows, :width] - total[rows:, width:]
    image_im = total[:rows, width:] + total[rows:, :width]
    map_re, map_im = maps_ref[0], maps_ref[1]
    grads[:, 0] = (map_re * image_re + map_im * image_im).reshape(views, row_block, width)
    grads[:, 1] = (map_re * image_im - map_im * image_re).reshape(views, row_block, width)
    copies = []
    for step in range(1, views):
        device = far[step - 1]
        copy = remote(
            grads.at[device["view"]],
            arrived.at[step],
            send_view.at[step],
            recv_view.at[step],
            device,
        )
        copy.start()
        copies.append(copy)
    out_ref[...] = grads[view]
    for step in range(1, views):
        copies[step - 1].wait_recv()
        out_ref[...] += arrived[step]
    for copy in copies + sends:
        copy.wait_send()


def coil_call(views, reps, gathered, maps, kspace, acquired, tables):
    rows, width = maps.shape[1:]
    vmem = pl.BlockSpec(memory_space=pltpu.VMEM)
    dma = pltpu.SemaphoreType.DMA
    return pl.pallas_call(
        functools.partial(coil_kernel, views, reps),
        out_shape=jax.ShapeDtypeStruct(gathered.shape[1:], f32),
        in_specs=[vmem] * 8,
        out_specs=vmem,
        scratch_shapes=[
            pltpu.VMEM((2, reps, rows, 2 * width), f32),
            pltpu.VMEM((2 * rows, 2 * width), f32),
            pltpu.VMEM((2, rows, width), f32),
            pltpu.VMEM(gathered.shape, f32),
            pltpu.VMEM(gathered.shape, f32),
            dma((4 * reps,)),
            dma((4 * reps,)),
            dma((views,)),
            dma((views,)),
        ],
        compiler_params=pltpu.CompilerParams(
            collective_id=1, has_side_effects=True, vmem_limit_bytes=48 * 1024 * 1024
        ),
        cost_estimate=pl.CostEstimate(
            flops=96 * rows * width * width,
            bytes_accessed=8 * gathered.size,
            transcendentals=0,
        ),
    )(gathered, maps, kspace, acquired, *tables)


def on_device(
    images,
    scaled_duals,
    proj_tiles,
    tile_ids,
    pixel_blocks,
    tof_offsets,
    counts,
    sinogram,
    coil_maps,
    kspace,
    sampling,
):
    rep_count = lax.axis_size("rep")
    view_count = lax.axis_size("view")
    owner_count = view_count * rep_count
    slab_count = lax.axis_size("slab")
    rep_at = lax.axis_index("rep")
    slab_at = lax.axis_index("slab")
    owner_at = lax.axis_index("view") * rep_count + rep_at
    row_block = images.shape[2]
    width = images.shape[3]
    tile_size = proj_tiles.shape[1]
    sectors, capacity = tile_ids.shape
    sector_bins = sinogram.shape[1] // sectors
    groups = coil_maps.shape[3]

    own_images = images[:, 0]
    ring = [(i, i + 1) for i in range(owner_count - 1)]
    row_after = lax.ppermute(own_images[:, :1], ("view", "rep"), [(b, a) for a, b in ring])
    chain = [(i, i + 1) for i in range(slab_count - 1)]
    slice_after = lax.ppermute(own_images, "slab", [(b, a) for a, b in chain])

    own_blocks = row_block * width // tile_size
    local = pixel_blocks - owner_at * own_blocks
    live = jnp.arange(capacity, dtype=jnp.int32)[None] < counts[:, None]
    local = jnp.where(live & (local >= 0) & (local < own_blocks), local, -1)
    start = tof_offsets + sector_bins * jnp.arange(sectors, dtype=jnp.int32)[:, None]
    chunk = 4 * capacity
    lists = [part.reshape(-1, 1, chunk) for part in (local, tile_ids, start)]
    info = jnp.concatenate(lists + [jnp.zeros_like(lists[0])] * 5, axis=1)
    pixel_rows = own_images[0].astype(bf16).reshape(-1, tile_size)
    bin_rows = sinogram.shape[1] // tile_size
    measured = sinogram[0].reshape(bin_rows, tile_size)
    gathered, pet_term = gather_call(
        view_count, rep_count, info, pixel_rows, proj_tiles, measured, own_images[1:3]
    )
    pet_term = pet_term.reshape(row_block, width)

    grid = np.arange(width)
    angle = (np.outer(grid, grid) % width) * (2.0 * np.pi / width)
    cosine, sine = np.cos(angle) / np.sqrt(width), np.sin(angle) / np.sqrt(width)
    by_rep = grid.reshape(groups, rep_count, row_block).transpose(1, 0, 2).reshape(rep_count, -1)
    row_tables = []
    for rep in range(rep_count):
        seen = np.concatenate([by_rep[(rep - step) % rep_count] for step in range(rep_count)])
        row_tables.append(
            np.concatenate([table[by_rep[rep]][:, seen] for table in (cosine, sine)], axis=0)
        )
    tables = [jnp.asarray(part) for part in split_table(np.concatenate([cosine, sine], axis=1))]
    for part in split_table(np.stack(row_tables)):
        tables.append(lax.dynamic_index_in_dim(jnp.asarray(part), rep_at, keepdims=False))
    rows = groups * row_block
    coil_gradient = coil_call(
        view_count,
        rep_count,
        gathered,
        coil_maps.reshape(2, rows, width),
        kspace.reshape(2, rows, width),
        sampling.reshape(rows, 1).astype(f32),
        tables,
    )
    data_gradient = jnp.concatenate([pet_term[None], coil_gradient], axis=0)

    global_rows = owner_at * row_block + jnp.arange(row_block, dtype=jnp.int32)
    row_keep = (global_rows < width - 1).astype(f32)[None, :, None]
    slice_keep = (slab_at < slab_count - 1).astype(f32)
    column_keep = (jnp.arange(width) < width - 1).astype(f32)[None, None, :]
    next_row = jnp.concatenate([own_images[:, 1:], row_after], axis=1)
    next_column = jnp.concatenate([own_images[..., 1:], own_images[..., :1]], axis=-1)
    diff_rows = (next_row - own_images) * row_keep
    diff_columns = (next_column - own_images) * column_keep
    diff_slices = (slice_after - own_images) * slice_keep
    differences = jnp.stack([diff_rows, diff_columns, diff_slices], axis=1).reshape(
        9, row_block, width
    )
    spread = differences + scaled_duals[:, 0]
    magnitude = jnp.sqrt(jnp.sum(spread * spread, axis=0))
    shrunk = spread * (jnp.maximum(magnitude - kappa, 0.0) / jnp.maximum(magnitude, kappa))[None]
    dual_next = spread - shrunk
    coupling = (differences - shrunk + dual_next).reshape(3, 3, row_block, width)
    couple_rows = coupling[:, 0] * row_keep
    couple_columns = coupling[:, 1] * column_keep
    couple_slices = coupling[:, 2] * slice_keep
    row_before = lax.ppermute(couple_rows[:, -1:], ("view", "rep"), ring)
    slice_before = lax.ppermute(couple_slices, "slab", chain)
    adjoint = (
        jnp.concatenate([row_before, couple_rows[:, :-1]], axis=1)
        - couple_rows
        + jnp.concatenate([couple_columns[..., -1:], couple_columns[..., :-1]], axis=-1)
        - couple_columns
        + slice_before
        - couple_slices
    )
    updated = own_images - step_size * (data_gradient + penalty * adjoint)
    return (updated[:, None], shrunk[:, None], dual_next[:, None])


def solution(mesh):
    placed = (
        P(None, ("grp", "slab"), ("view", "rep"), None),
        P(None, ("grp", "slab"), ("view", "rep"), None),
        P(),
        P(),
        P(),
        P(),
        P(),
        P(("grp", "slab"), None),
        P(None, "view", ("grp", "slab"), None, "rep", None, None),
        P(None, "view", ("grp", "slab"), None, "rep", None, None),
        P(("grp", "slab"), None, "rep", None),
    )
    return jax.shard_map(
        on_device,
        mesh=mesh,
        in_specs=placed,
        out_specs=(
            P(None, ("grp", "slab"), ("view", "rep"), None),
            P(None, ("grp", "slab"), ("view", "rep"), None),
            P(None, ("grp", "slab"), ("view", "rep"), None),
        ),
        check_vma=False,
    )
```

```python
import functools
import math

import jax
import jax.numpy as jnp
import ml_dtypes
import numpy as np
from jax import lax
from jax.experimental import pallas as pl
from jax.experimental.pallas import tpu as pltpu
from jax.sharding import PartitionSpec as P

kappa = 4.0
step_size = 0.4
penalty = 0.5
bf16 = jnp.bfloat16
f32 = jnp.float32


def contract(left, right, left_dim, right_dim):
    return lax.dot_general(
        left, right, (((left_dim,), (right_dim,)), ((), ())), preferred_element_type=f32
    )


def split_table(table):
    high = table.astype(ml_dtypes.bfloat16)
    low = (table - high.astype(np.float64)).astype(ml_dtypes.bfloat16)
    return high, low


def split_data(values):
    high = values.astype(bf16)
    return high, (values - high.astype(f32)).astype(bf16)


def one_hot(count, index):
    rows = lax.broadcasted_iota(jnp.int32, (count, index.shape[1]), 0)
    return jnp.where(rows == index, 1.0, 0.0).astype(bf16)


def masked_pair(values, ids, pair):
    parts = []
    for which in range(2):
        flag = jnp.where(ids == 2 * pair + which, 1.0, 0.0).astype(bf16)
        parts.append(values * flag)
    return jnp.concatenate(parts, axis=0)


def project(info_ref, at, rows_ref, tiles_ref, sino_ref, total):
    local, ids, start = info_ref[at, 0:1], info_ref[at, 1:2], info_ref[at, 2:3]
    tile = tiles_ref.shape[1]
    pixels = contract(rows_ref[...], one_hot(rows_ref.shape[0], local), 0, 0).astype(bf16)
    total[...] = jnp.zeros_like(total)

    def step(pair, carry):
        tiles = jnp.concatenate([tiles_ref[2 * pair], tiles_ref[2 * pair + 1]], axis=1)
        total[...] += contract(tiles, masked_pair(pixels, ids, pair), 1, 0)
        return carry

    lax.fori_loop(0, tiles_ref.shape[0] // 2, step, 0)
    moved = jnp.concatenate([total[...], jnp.zeros_like(total)], axis=0)
    shift = start % tile
    for bit in range(int(math.log2(tile))):
        moved = jnp.where((shift >> bit) & 1 == 1, pltpu.roll(moved, 1 << bit, 0), moved)
    bins = start // tile
    rows = sino_ref.shape[0]
    for half in range(2):
        place = one_hot(rows, bins + half)
        rest = moved[half * tile : (half + 1) * tile]
        for _ in range(3):
            part = rest.astype(bf16)
            sino_ref[...] += contract(place, part, 1, 1)
            rest = rest - part.astype(f32)


def back_project(info_ref, at, resid, tiles_ref, back_ref, total):
    local, ids, start = info_ref[at, 0:1], info_ref[at, 1:2], info_ref[at, 2:3]
    tile = tiles_ref.shape[1]
    bins = start // tile
    shift = start % tile
    moved = jnp.concatenate(
        [contract(resid, one_hot(resid.shape[0], bins + half), 0, 0) for half in range(2)], axis=0
    )
    for bit in range(int(math.log2(tile))):
        moved = jnp.where(
            (shift >> bit) & 1 == 1, pltpu.roll(moved, 2 * tile - (1 << bit), 0), moved
        )
    window = moved[:tile].astype(bf16)
    total[...] = jnp.zeros_like(total)

    def step(pair, carry):
        tiles = jnp.concatenate([tiles_ref[2 * pair], tiles_ref[2 * pair + 1]], axis=0)
        total[...] += contract(tiles, masked_pair(window, ids, pair), 0, 0)
        return carry

    lax.fori_loop(0, tiles_ref.shape[0] // 2, step, 0)
    place = one_hot(back_ref.shape[0], local)
    rest = total[...]
    for _ in range(3):
        part = rest.astype(bf16)
        back_ref[...] += contract(place, part, 1, 1)
        rest = rest - part.astype(f32)


MESH = pl.DeviceIdType.MESH


def remote(source, target, send_sem, recv_sem, device):
    return pltpu.make_async_remote_copy(
        src_ref=source,
        dst_ref=target,
        send_sem=send_sem,
        recv_sem=recv_sem,
        device_id=device,
        device_id_type=MESH,
    )


def greet(devices):
    barrier = pltpu.get_barrier_semaphore()
    for device in devices:
        pl.semaphore_signal(barrier, inc=1, device_id=device, device_id_type=MESH)
    pl.semaphore_wait(barrier, len(devices))


def split_product(left, right):
    return (
        contract(left[0], right[0], 1, 0)
        + contract(left[1], right[0], 1, 0)
        + contract(left[0], right[1], 1, 0)
    )


def step_kernel(
    views,
    reps,
    slabs,
    info_ref,
    rows_ref,
    measured_ref,
    images_ref,
    acquired_ref,
    tiles_hbm,
    duals_hbm,
    maps_hbm,
    kspace_hbm,
    column_high_hbm,
    column_low_hbm,
    row_high_hbm,
    row_low_hbm,
    updated_ref,
    shrunk_ref,
    dual_ref,
    tiles_ref,
    duals_ref,
    maps_ref,
    kspace_ref,
    column_high,
    column_low,
    row_high,
    row_low,
    load_sems,
    slots_total,
    sino,
    slots,
    back,
    gathered,
    buffers,
    total,
    resid,
    grads,
    arrived,
    couple,
    row_after,
    slice_after,
    row_before,
    slice_before,
    send_halo,
    recv_halo,
    send_rows,
    recv_rows,
    send_sino,
    recv_sino,
    send_rep,
    recv_rep,
    send_view,
    recv_view,
):
    view, rep, slab = lax.axis_index("view"), lax.axis_index("rep"), lax.axis_index("slab")
    count = views * reps
    me = view * reps + rep
    rows, width = maps_ref.shape[1], maps_ref.shape[2]
    row_block = images_ref.shape[1]

    pairs = [
        (tiles_hbm, tiles_ref),
        (duals_hbm, duals_ref),
        (maps_hbm, maps_ref),
        (column_high_hbm, column_high),
        (column_low_hbm, column_low),
        (row_high_hbm.at[rep], row_high),
        (row_low_hbm.at[rep], row_low),
        (kspace_hbm, kspace_ref),
    ]
    loads = [
        pltpu.make_async_copy(source, target, load_sems.at[at])
        for at, (source, target) in enumerate(pairs)
    ]
    for load in loads:
        load.start()

    def owner(index):
        index = lax.rem(index, count)
        return {"view": index // reps, "rep": lax.rem(index, reps), "slab": slab}

    def other_slab(step):
        return {"view": view, "rep": rep, "slab": lax.rem(slab + step, slabs)}

    near = [owner(view * reps + lax.rem(rep + step, reps)) for step in range(1, reps)]
    far = [owner(lax.rem(view + step, views) * reps + rep) for step in range(1, views)]
    side = [other_slab(step) for step in sorted({1, slabs - 1})]
    greet([owner(me + step) for step in range(1, count)] + side)
    halos = [
        remote(
            images_ref.at[:, 0:8], row_after, send_halo.at[0], recv_halo.at[0], owner(me + count - 1)
        ),
        remote(images_ref, slice_after, send_halo.at[1], recv_halo.at[1], other_slab(slabs - 1)),
        remote(
            couple.at[0, :, row_block - 8 : row_block],
            row_before,
            send_halo.at[2],
            recv_halo.at[2],
            owner(me + 1),
        ),
        remote(couple.at[2], slice_before, send_halo.at[3], recv_halo.at[3], other_slab(1)),
    ]
    halos[0].start()
    halos[1].start()
    own_mr = images_ref.at[1:3]
    moves = []
    for step in range(views - 1, 0, -1):
        copy = remote(
            own_mr, gathered.at[view], send_rows.at[step], recv_rows.at[step], far[step - 1]
        )
        copy.start()
        moves.append(copy)
    gathered[view] = images_ref[1:3]

    sino[...] = jnp.zeros_like(sino)
    loads[0].wait()
    for at in range(info_ref.shape[0]):
        project(info_ref, at, rows_ref, tiles_ref, sino, slots_total)
    sums = []
    for step in range(1, count):
        copy = remote(
            sino, slots.at[step], send_sino.at[step], recv_sino.at[step], owner(me + step)
        )
        copy.start()
        sums.append(copy)

    halos[0].wait_recv()
    halos[1].wait_recv()
    loads[1].wait()
    shape = (row_block, width)
    global_rows = lax.broadcasted_iota(jnp.int32, shape, 0) + me * row_block
    row_keep = jnp.where(global_rows < width - 1, 1.0, 0.0)
    column_keep = jnp.where(lax.broadcasted_iota(jnp.int32, shape, 1) < width - 1, 1.0, 0.0)
    slice_keep = jnp.where(slab < slabs - 1, 1.0, 0.0)
    keeps = (row_keep, column_keep, slice_keep)
    squares = jnp.zeros(shape, f32)
    for channel in range(3):
        own = images_ref[channel]
        nexts = (
            jnp.concatenate([own[1:], row_after[channel, 0:1]], axis=0),
            pltpu.roll(own, width - 1, 1),
            slice_after[channel],
        )
        for way in range(3):
            difference = (nexts[way] - own) * keeps[way]
            spread = difference + duals_ref[3 * channel + way]
            couple[way, channel] = difference
            dual_ref[3 * channel + way] = spread
            squares += spread * spread
    magnitude = jnp.sqrt(squares)
    factor = jnp.maximum(magnitude - kappa, 0.0) / jnp.maximum(magnitude, kappa)
    for channel in range(3):
        for way in range(3):
            spread = dual_ref[3 * channel + way]
            shrunk = spread * factor
            dual = spread - shrunk
            shrunk_ref[3 * channel + way] = shrunk
            dual_ref[3 * channel + way] = dual
            couple[way, channel] = (couple[way, channel] - shrunk + dual) * keeps[way]
    halos[2].start()
    halos[3].start()

    halves = 2
    part = rows // halves
    sends = []

    def columns(stage, half, real, imag, sign):
        table = (column_high[...], column_low[...])
        out = split_product(split_data(jnp.concatenate([real, imag], axis=0)), table)
        where = pl.ds(half * part, part)
        buffers[stage, 0, where, :width] = out[:part, :width] + sign * out[part:, width:]
        buffers[stage, 0, where, width:] = out[part:, :width] - sign * out[:part, width:]
        for step in range(1, reps):
            index = (stage * halves + half) * reps + step
            copy = remote(
                buffers.at[stage, 0, where],
                buffers.at[stage, step, where],
                send_rep.at[index],
                recv_rep.at[index],
                near[step - 1],
            )
            copy.start()
            sends.append(copy)

    def row_products(stage):
        for step in range(reps):
            if step:
                for half in range(halves):
                    sends[(stage * halves + half) * (reps - 1) + step - 1].wait_recv()
            where = pl.ds(step * rows, rows)
            table = (row_high[:, where], row_low[:, where])
            product = split_product(table, split_data(buffers[stage, step]))
            if step:
                total[...] += product
            else:
                total[...] = product

    for load in loads[2:]:
        load.wait()
    for step in range(1, views):
        source = lax.rem(view + views - step, views)
        remote(
            own_mr,
            gathered.at[source],
            send_rows.at[step],
            recv_rows.at[step],
            owner(source * reps + rep),
        ).wait_recv()
    blocks = part // row_block
    for half in range(halves):
        where = pl.ds(half * part, part)
        real = gathered[half * blocks : (half + 1) * blocks, 0].reshape(part, width)
        imag = gathered[half * blocks : (half + 1) * blocks, 1].reshape(part, width)
        map_re, map_im = maps_ref[0, where], maps_ref[1, where]
        columns(0, half, map_re * real - map_im * imag, map_re * imag + map_im * real, 1.0)
    row_products(0)
    acquired = acquired_ref[...]
    resid[0] = acquired * (total[:rows, :width] + total[rows:, width:] - kspace_ref[0])
    resid[1] = acquired * (total[:rows, width:] - total[rows:, :width] - kspace_ref[1])
    for half in range(halves):
        where = pl.ds(half * part, part)
        columns(1, half, resid[0, where], resid[1, where], -1.0)
    row_products(1)
    image_re = total[:rows, :width] - total[rows:, width:]
    image_im = total[:rows, width:] + total[rows:, :width]
    map_re, map_im = maps_ref[0], maps_ref[1]
    grads[:, 0] = (map_re * image_re + map_im * image_im).reshape(views, row_block, width)
    grads[:, 1] = (map_re * image_im - map_im * image_re).reshape(views, row_block, width)
    copies = []
    for step in range(1, views):
        device = far[step - 1]
        copy = remote(
            grads.at[device["view"]],
            arrived.at[step],
            send_view.at[step],
            recv_view.at[step],
            device,
        )
        copy.start()
        copies.append(copy)

    for copy in sums:
        copy.wait()
    full = sino[...]
    for step in range(1, count):
        full = full + slots[step]
    pet_residual = (full - measured_ref[...].astype(f32)).astype(bf16)
    back[...] = jnp.zeros_like(back)
    for at in range(info_ref.shape[0]):
        back_project(info_ref, at, pet_residual, tiles_ref, back, slots_total)

    halos[2].wait_recv()
    halos[3].wait_recv()
    per_row = width // back.shape[1]
    for channel in range(3):
        across = couple[0, channel]
        along = couple[1, channel]
        adjoint = (
            jnp.concatenate([row_before[channel, 7:8], across[:-1]], axis=0)
            - across
            + pltpu.roll(along, 1, 1)
            - along
            + slice_before[channel]
            - couple[2, channel]
        )
        if channel:
            gradient = grads[view, channel - 1]
        else:
            gradient = back[...].reshape(row_block, per_row, back.shape[1]).reshape(shape)
        updated_ref[channel] = images_ref[channel] - step_size * (gradient + penalty * adjoint)
    for step in range(1, views):
        copies[step - 1].wait_recv()
        updated_ref[1:3] += -step_size * arrived[step]
    for copy in moves + copies + sends + halos:
        copy.wait_send()


def step_call(mesh_sizes, staged, loaded):
    views, reps, slabs = mesh_sizes
    info, rows_in, measured, images, acquired = staged
    tiles, duals, maps, kspace = loaded[:4]
    chunk = info.shape[2]
    tile = tiles.shape[1]
    rows, width = maps.shape[1:]
    count = views * reps
    vmem = pl.BlockSpec(memory_space=pltpu.VMEM)
    dma = pltpu.SemaphoreType.DMA
    held = [pltpu.VMEM(value.shape, value.dtype) for value in loaded[:6]]
    held += [pltpu.VMEM(value.shape[1:], value.dtype) for value in loaded[6:]]
    pieces = (views, 2, *images.shape[1:])
    edge = (3, 8, width)
    return pl.pallas_call(
        functools.partial(step_kernel, views, reps, slabs),
        out_shape=(
            jax.ShapeDtypeStruct(images.shape, f32),
            jax.ShapeDtypeStruct(duals.shape, f32),
            jax.ShapeDtypeStruct(duals.shape, f32),
        ),
        in_specs=[vmem] * len(staged) + [pl.BlockSpec(memory_space=pl.ANY)] * len(loaded),
        out_specs=(vmem, vmem, vmem),
        scratch_shapes=held
        + [
            dma((len(loaded),)),
            pltpu.VMEM((tile, chunk), f32),
            pltpu.VMEM(measured.shape, f32),
            pltpu.VMEM((count, *measured.shape), f32),
            pltpu.VMEM(rows_in.shape, f32),
            pltpu.VMEM(pieces, f32),
            pltpu.VMEM((2, reps, rows, 2 * width), f32),
            pltpu.VMEM((2 * rows, 2 * width), f32),
            pltpu.VMEM((2, rows, width), f32),
            pltpu.VMEM(pieces, f32),
            pltpu.VMEM(pieces, f32),
            pltpu.VMEM((3, *images.shape), f32),
            pltpu.VMEM(edge, f32),
            pltpu.VMEM(images.shape, f32),
            pltpu.VMEM(edge, f32),
            pltpu.VMEM(images.shape, f32),
            dma((4,)),
            dma((4,)),
            dma((views,)),
            dma((views,)),
            dma((count,)),
            dma((count,)),
            dma((4 * reps,)),
            dma((4 * reps,)),
            dma((views,)),
            dma((views,)),
        ],
        compiler_params=pltpu.CompilerParams(
            collective_id=0, has_side_effects=True, vmem_limit_bytes=60 * 1024 * 1024
        ),
    )(*staged, *loaded)


def on_device(
    images,
    scaled_duals,
    proj_tiles,
    tile_ids,
    pixel_blocks,
    tof_offsets,
    counts,
    sinogram,
    coil_maps,
    kspace,
    sampling,
):
    rep_count = lax.axis_size("rep")
    view_count = lax.axis_size("view")
    owner_count = view_count * rep_count
    slab_count = lax.axis_size("slab")
    owner_at = lax.axis_index("view") * rep_count + lax.axis_index("rep")
    row_block = images.shape[2]
    width = images.shape[3]
    tile_size = proj_tiles.shape[1]
    sectors, capacity = tile_ids.shape
    sector_bins = sinogram.shape[1] // sectors
    groups = coil_maps.shape[3]

    own_images = images[:, 0]

    own_blocks = row_block * width // tile_size
    local = pixel_blocks - owner_at * own_blocks
    live = jnp.arange(capacity, dtype=jnp.int32)[None] < counts[:, None]
    local = jnp.where(live & (local >= 0) & (local < own_blocks), local, -1)
    start = tof_offsets + sector_bins * jnp.arange(sectors, dtype=jnp.int32)[:, None]
    chunk = 4 * capacity
    lists = [part.reshape(-1, 1, chunk) for part in (local, tile_ids, start)]
    info = jnp.concatenate(lists + [jnp.zeros_like(lists[0])] * 5, axis=1)
    pixel_rows = own_images[0].astype(bf16).reshape(-1, tile_size)
    bin_rows = sinogram.shape[1] // tile_size
    measured = sinogram[0].reshape(bin_rows, tile_size)
    grid = np.arange(width)
    angle = (np.outer(grid, grid) % width) * (2.0 * np.pi / width)
    cosine, sine = np.cos(angle) / np.sqrt(width), np.sin(angle) / np.sqrt(width)
    by_rep = grid.reshape(groups, rep_count, row_block).transpose(1, 0, 2).reshape(rep_count, -1)
    row_tables = []
    for rep in range(rep_count):
        seen = np.concatenate([by_rep[(rep - step) % rep_count] for step in range(rep_count)])
        row_tables.append(
            np.concatenate([table[by_rep[rep]][:, seen] for table in (cosine, sine)], axis=0)
        )
    tables = [jnp.asarray(part) for part in split_table(np.concatenate([cosine, sine], axis=1))]
    tables += [jnp.asarray(part) for part in split_table(np.stack(row_tables))]
    rows = groups * row_block
    updated, shrunk, dual_next = step_call(
        (view_count, rep_count, slab_count),
        (info, pixel_rows, measured, own_images, sampling.reshape(rows, 1).astype(f32)),
        (
            proj_tiles,
            scaled_duals[:, 0],
            coil_maps.reshape(2, rows, width),
            kspace.reshape(2, rows, width),
            *tables,
        ),
    )
    return (updated[:, None], shrunk[:, None], dual_next[:, None])


def solution(mesh):
    placed = (
        P(None, ("grp", "slab"), ("view", "rep"), None),
        P(None, ("grp", "slab"), ("view", "rep"), None),
        P(),
        P(),
        P(),
        P(),
        P(),
        P(("grp", "slab"), None),
        P(None, "view", ("grp", "slab"), None, "rep", None, None),
        P(None, "view", ("grp", "slab"), None, "rep", None, None),
        P(("grp", "slab"), None, "rep", None),
    )
    return jax.shard_map(
        on_device,
        mesh=mesh,
        in_specs=placed,
        out_specs=(
            P(None, ("grp", "slab"), ("view", "rep"), None),
            P(None, ("grp", "slab"), ("view", "rep"), None),
            P(None, ("grp", "slab"), ("view", "rep"), None),
        ),
        check_vma=False,
    )
```

```python
import functools
import math

import jax
import jax.numpy as jnp
import ml_dtypes
import numpy as np
from jax import lax
from jax.experimental import pallas as pl
from jax.experimental.pallas import tpu as pltpu
from jax.sharding import PartitionSpec as P

kappa = 4.0
step_size = 0.4
penalty = 0.5
bf16 = jnp.bfloat16
f32 = jnp.float32


def contract(left, right, left_dim, right_dim):
    return lax.dot_general(
        left, right, (((left_dim,), (right_dim,)), ((), ())), preferred_element_type=f32
    )


def split_table(table):
    high = table.astype(ml_dtypes.bfloat16)
    low = (table - high.astype(np.float64)).astype(ml_dtypes.bfloat16)
    return high, low


def split_data(values):
    high = values.astype(bf16)
    return high, (values - high.astype(f32)).astype(bf16)


def one_hot(count, index):
    rows = lax.broadcasted_iota(jnp.int32, (count, index.shape[1]), 0)
    return jnp.where(rows == index, 1.0, 0.0).astype(bf16)


def masked_pair(values, ids, pair):
    parts = []
    for which in range(2):
        flag = jnp.where(ids == 2 * pair + which, 1.0, 0.0).astype(bf16)
        parts.append(values * flag)
    return jnp.concatenate(parts, axis=0)


def project(info_ref, at, rows_ref, tiles_ref, sino_ref, total):
    local, ids, start = info_ref[at, 0:1], info_ref[at, 1:2], info_ref[at, 2:3]
    tile = tiles_ref.shape[1]
    pixels = contract(rows_ref[...], one_hot(rows_ref.shape[0], local), 0, 0).astype(bf16)
    total[...] = jnp.zeros_like(total)

    def step(pair, carry):
        tiles = jnp.concatenate([tiles_ref[2 * pair], tiles_ref[2 * pair + 1]], axis=1)
        total[...] += contract(tiles, masked_pair(pixels, ids, pair), 1, 0)
        return carry

    lax.fori_loop(0, tiles_ref.shape[0] // 2, step, 0)
    moved = jnp.concatenate([total[...], jnp.zeros_like(total)], axis=0)
    shift = start % tile
    for bit in range(int(math.log2(tile))):
        moved = jnp.where((shift >> bit) & 1 == 1, pltpu.roll(moved, 1 << bit, 0), moved)
    bins = start // tile
    rows = sino_ref.shape[0]
    for half in range(2):
        place = one_hot(rows, bins + half)
        rest = moved[half * tile : (half + 1) * tile]
        for _ in range(3):
            part = rest.astype(bf16)
            sino_ref[...] += contract(place, part, 1, 1)
            rest = rest - part.astype(f32)


def back_project(info_ref, at, resid, tiles_ref, back_ref, total):
    local, ids, start = info_ref[at, 0:1], info_ref[at, 1:2], info_ref[at, 2:3]
    tile = tiles_ref.shape[1]
    bins = start // tile
    shift = start % tile
    moved = jnp.concatenate(
        [contract(resid, one_hot(resid.shape[0], bins + half), 0, 0) for half in range(2)], axis=0
    )
    for bit in range(int(math.log2(tile))):
        moved = jnp.where(
            (shift >> bit) & 1 == 1, pltpu.roll(moved, 2 * tile - (1 << bit), 0), moved
        )
    window = moved[:tile].astype(bf16)
    total[...] = jnp.zeros_like(total)

    def step(pair, carry):
        tiles = jnp.concatenate([tiles_ref[2 * pair], tiles_ref[2 * pair + 1]], axis=0)
        total[...] += contract(tiles, masked_pair(window, ids, pair), 0, 0)
        return carry

    lax.fori_loop(0, tiles_ref.shape[0] // 2, step, 0)
    place = one_hot(back_ref.shape[0], local)
    rest = total[...]
    for _ in range(3):
        part = rest.astype(bf16)
        back_ref[...] += contract(place, part, 1, 1)
        rest = rest - part.astype(f32)


MESH = pl.DeviceIdType.MESH


def remote(source, target, send_sem, recv_sem, device):
    return pltpu.make_async_remote_copy(
        src_ref=source,
        dst_ref=target,
        send_sem=send_sem,
        recv_sem=recv_sem,
        device_id=device,
        device_id_type=MESH,
    )


def greet(devices):
    barrier = pltpu.get_barrier_semaphore()
    for device in devices:
        pl.semaphore_signal(barrier, inc=1, device_id=device, device_id_type=MESH)
    pl.semaphore_wait(barrier, len(devices))


def split_product(left, right):
    return (
        contract(left[0], right[0], 1, 0)
        + contract(left[1], right[0], 1, 0)
        + contract(left[0], right[1], 1, 0)
    )


def step_kernel(
    views,
    reps,
    slabs,
    counts_ref,
    ids_ref,
    blocks_ref,
    offsets_ref,
    sinogram_ref,
    images_ref,
    sampling_ref,
    tiles_hbm,
    duals_hbm,
    maps_hbm,
    kspace_hbm,
    column_high_hbm,
    column_low_hbm,
    row_high_hbm,
    row_low_hbm,
    updated_ref,
    shrunk_ref,
    dual_ref,
    tiles_ref,
    duals_ref,
    maps_ref,
    kspace_ref,
    column_high,
    column_low,
    row_high,
    row_low,
    load_sems,
    info_ref,
    rows_ref,
    measured_ref,
    acquired_ref,
    slots_total,
    sino,
    slots,
    back,
    gathered,
    buffers,
    total,
    resid,
    grads,
    arrived,
    couple,
    row_after,
    slice_after,
    row_before,
    slice_before,
    send_halo,
    recv_halo,
    send_rows,
    recv_rows,
    send_sino,
    recv_sino,
    send_rep,
    recv_rep,
    send_view,
    recv_view,
):
    view, rep, slab = lax.axis_index("view"), lax.axis_index("rep"), lax.axis_index("slab")
    count = views * reps
    me = view * reps + rep
    rows, width = maps_ref.shape[1], maps_ref.shape[2]
    row_block = images_ref.shape[1]

    pairs = [
        (tiles_hbm, tiles_ref),
        (duals_hbm, duals_ref),
        (maps_hbm, maps_ref),
        (column_high_hbm, column_high),
        (column_low_hbm, column_low),
        (row_high_hbm.at[rep], row_high),
        (row_low_hbm.at[rep], row_low),
        (kspace_hbm, kspace_ref),
    ]
    loads = [
        pltpu.make_async_copy(source, target, load_sems.at[at])
        for at, (source, target) in enumerate(pairs)
    ]
    for load in loads:
        load.start()

    def owner(index):
        index = lax.rem(index, count)
        return {"view": index // reps, "rep": lax.rem(index, reps), "slab": slab}

    def other_slab(step):
        return {"view": view, "rep": rep, "slab": lax.rem(slab + step, slabs)}

    near = [owner(view * reps + lax.rem(rep + step, reps)) for step in range(1, reps)]
    far = [owner(lax.rem(view + step, views) * reps + rep) for step in range(1, views)]
    side = [other_slab(step) for step in sorted({1, slabs - 1})]
    greet([owner(me + step) for step in range(1, count)] + side)
    halos = [
        remote(
            images_ref.at[:, 0:8], row_after, send_halo.at[0], recv_halo.at[0], owner(me + count - 1)
        ),
        remote(images_ref, slice_after, send_halo.at[1], recv_halo.at[1], other_slab(slabs - 1)),
        remote(
            couple.at[0, :, row_block - 8 : row_block],
            row_before,
            send_halo.at[2],
            recv_halo.at[2],
            owner(me + 1),
        ),
        remote(couple.at[2], slice_before, send_halo.at[3], recv_halo.at[3], other_slab(1)),
    ]
    halos[0].start()
    halos[1].start()
    own_mr = images_ref.at[1:3]
    moves = []
    for step in range(views - 1, 0, -1):
        copy = remote(
            own_mr, gathered.at[view], send_rows.at[step], recv_rows.at[step], far[step - 1]
        )
        copy.start()
        moves.append(copy)
    gathered[view] = images_ref[1:3]

    sectors, capacity = ids_ref.shape
    per_chunk = sectors // info_ref.shape[0]
    tile = tiles_ref.shape[1]
    own_blocks = rows_ref.shape[0]
    sector_bins = sinogram_ref.shape[1] // sectors
    for sector in range(sectors):
        at, lanes = sector // per_chunk, pl.ds(sector % per_chunk * capacity, capacity)
        pick = slice(sector, sector + 1)
        local = blocks_ref[pick] - me * own_blocks
        slot = lax.broadcasted_iota(jnp.int32, (1, capacity), 1)
        live = (slot < counts_ref[sector]) & (local >= 0) & (local < own_blocks)
        info_ref[at, 0:1, lanes] = jnp.where(live, local, -1)
        info_ref[at, 1:2, lanes] = ids_ref[pick]
        info_ref[at, 2:3, lanes] = offsets_ref[pick] + sector * sector_bins
    rows_ref[...] = (
        images_ref[0]
        .reshape(row_block, width // tile, tile)
        .reshape(own_blocks, tile)
        .astype(bf16)
    )

    sino[...] = jnp.zeros_like(sino)
    loads[0].wait()
    for at in range(info_ref.shape[0]):
        project(info_ref, at, rows_ref, tiles_ref, sino, slots_total)
    sums = []
    for step in range(1, count):
        copy = remote(
            sino, slots.at[step], send_sino.at[step], recv_sino.at[step], owner(me + step)
        )
        copy.start()
        sums.append(copy)

    measured = sinogram_ref[...].astype(f32)
    for row in range(measured_ref.shape[0]):
        measured_ref[row : row + 1] = measured[:, row * tile : (row + 1) * tile]
    square = (row_block, row_block)
    diagonal = lax.broadcasted_iota(jnp.int32, square, 0) == lax.broadcasted_iota(
        jnp.int32, square, 1
    )
    for group in range(rows // row_block):
        flags = sampling_ref[group : group + 1].astype(f32)
        acquired_ref[group * row_block : (group + 1) * row_block] = jnp.sum(
            jnp.where(diagonal, flags, 0.0), axis=1, keepdims=True
        )

    halos[0].wait_recv()
    halos[1].wait_recv()
    loads[1].wait()
    shape = (row_block, width)
    global_rows = lax.broadcasted_iota(jnp.int32, shape, 0) + me * row_block
    row_keep = jnp.where(global_rows < width - 1, 1.0, 0.0)
    column_keep = jnp.where(lax.broadcasted_iota(jnp.int32, shape, 1) < width - 1, 1.0, 0.0)
    slice_keep = jnp.where(slab < slabs - 1, 1.0, 0.0)
    keeps = (row_keep, column_keep, slice_keep)
    squares = jnp.zeros(shape, f32)
    for channel in range(3):
        own = images_ref[channel]
        nexts = (
            jnp.concatenate([own[1:], row_after[channel, 0:1]], axis=0),
            pltpu.roll(own, width - 1, 1),
            slice_after[channel],
        )
        for way in range(3):
            difference = (nexts[way] - own) * keeps[way]
            spread = difference + duals_ref[3 * channel + way]
            couple[way, channel] = difference
            dual_ref[3 * channel + way] = spread
            squares += spread * spread
    magnitude = jnp.sqrt(squares)
    factor = jnp.maximum(magnitude - kappa, 0.0) / jnp.maximum(magnitude, kappa)
    for channel in range(3):
        for way in range(3):
            spread = dual_ref[3 * channel + way]
            shrunk = spread * factor
            dual = spread - shrunk
            shrunk_ref[3 * channel + way] = shrunk
            dual_ref[3 * channel + way] = dual
            couple[way, channel] = (couple[way, channel] - shrunk + dual) * keeps[way]
    halos[2].start()
    halos[3].start()

    halves = 2
    part = rows // halves
    sends = []

    def columns(stage, half, real, imag, sign):
        table = (column_high[...], column_low[...])
        out = split_product(split_data(jnp.concatenate([real, imag], axis=0)), table)
        where = pl.ds(half * part, part)
        buffers[stage, 0, where, :width] = out[:part, :width] + sign * out[part:, width:]
        buffers[stage, 0, where, width:] = out[part:, :width] - sign * out[:part, width:]
        for step in range(1, reps):
            index = (stage * halves + half) * reps + step
            copy = remote(
                buffers.at[stage, 0, where],
                buffers.at[stage, step, where],
                send_rep.at[index],
                recv_rep.at[index],
                near[step - 1],
            )
            copy.start()
            sends.append(copy)

    def row_products(stage):
        for step in range(reps):
            if step:
                for half in range(halves):
                    sends[(stage * halves + half) * (reps - 1) + step - 1].wait_recv()
            where = pl.ds(step * rows, rows)
            table = (row_high[:, where], row_low[:, where])
            product = split_product(table, split_data(buffers[stage, step]))
            if step:
                total[...] += product
            else:
                total[...] = product

    for load in loads[2:]:
        load.wait()
    for step in range(1, views):
        source = lax.rem(view + views - step, views)
        remote(
            own_mr,
            gathered.at[source],
            send_rows.at[step],
            recv_rows.at[step],
            owner(source * reps + rep),
        ).wait_recv()
    blocks = part // row_block
    for half in range(halves):
        where = pl.ds(half * part, part)
        real = gathered[half * blocks : (half + 1) * blocks, 0].reshape(part, width)
        imag = gathered[half * blocks : (half + 1) * blocks, 1].reshape(part, width)
        map_re, map_im = maps_ref[0, where], maps_ref[1, where]
        columns(0, half, map_re * real - map_im * imag, map_re * imag + map_im * real, 1.0)
    row_products(0)
    acquired = acquired_ref[...]
    resid[0] = acquired * (total[:rows, :width] + total[rows:, width:] - kspace_ref[0])
    resid[1] = acquired * (total[:rows, width:] - total[rows:, :width] - kspace_ref[1])
    for half in range(halves):
        where = pl.ds(half * part, part)
        columns(1, half, resid[0, where], resid[1, where], -1.0)
    row_products(1)
    image_re = total[:rows, :width] - total[rows:, width:]
    image_im = total[:rows, width:] + total[rows:, :width]
    map_re, map_im = maps_ref[0], maps_ref[1]
    grads[:, 0] = (map_re * image_re + map_im * image_im).reshape(views, row_block, width)
    grads[:, 1] = (map_re * image_im - map_im * image_re).reshape(views, row_block, width)
    copies = []
    for step in range(1, views):
        device = far[step - 1]
        copy = remote(
            grads.at[device["view"]],
            arrived.at[step],
            send_view.at[step],
            recv_view.at[step],
            device,
        )
        copy.start()
        copies.append(copy)

    for copy in sums:
        copy.wait()
    full = sino[...]
    for step in range(1, count):
        full = full + slots[step]
    pet_residual = (full - measured_ref[...]).astype(bf16)
    back[...] = jnp.zeros_like(back)
    for at in range(info_ref.shape[0]):
        back_project(info_ref, at, pet_residual, tiles_ref, back, slots_total)

    halos[2].wait_recv()
    halos[3].wait_recv()
    per_row = width // back.shape[1]
    for channel in range(3):
        across = couple[0, channel]
        along = couple[1, channel]
        adjoint = (
            jnp.concatenate([row_before[channel, 7:8], across[:-1]], axis=0)
            - across
            + pltpu.roll(along, 1, 1)
            - along
            + slice_before[channel]
            - couple[2, channel]
        )
        if channel:
            gradient = grads[view, channel - 1]
        else:
            gradient = back[...].reshape(row_block, per_row, back.shape[1]).reshape(shape)
        updated_ref[channel] = images_ref[channel] - step_size * (gradient + penalty * adjoint)
    for step in range(1, views):
        copies[step - 1].wait_recv()
        updated_ref[1:3] += -step_size * arrived[step]
    for copy in moves + copies + sends + halos:
        copy.wait_send()


def step_call(mesh_sizes, staged, loaded):
    views, reps, slabs = mesh_sizes
    counts, ids, _, _, sinogram, images, _ = staged
    tiles, duals, maps, kspace = loaded[:4]
    sectors, capacity = ids.shape
    per_chunk = min(4, sectors)
    chunk = per_chunk * capacity
    tile = tiles.shape[1]
    rows, width = maps.shape[1:]
    count = views * reps
    own_shape = (images.shape[1] * width // tile, tile)
    bins_shape = (sinogram.shape[1] // tile, tile)
    vmem = pl.BlockSpec(memory_space=pltpu.VMEM)
    dma = pltpu.SemaphoreType.DMA
    held = [pltpu.VMEM(value.shape, value.dtype) for value in loaded[:6]]
    held += [pltpu.VMEM(value.shape[1:], value.dtype) for value in loaded[6:]]
    pieces = (views, 2, *images.shape[1:])
    edge = (3, 8, width)
    return pl.pallas_call(
        functools.partial(step_kernel, views, reps, slabs),
        out_shape=(
            jax.ShapeDtypeStruct(images.shape, f32),
            jax.ShapeDtypeStruct(duals.shape, f32),
            jax.ShapeDtypeStruct(duals.shape, f32),
        ),
        in_specs=[pl.BlockSpec(memory_space=pltpu.SMEM)]
        + [vmem] * (len(staged) - 1)
        + [pl.BlockSpec(memory_space=pl.ANY)] * len(loaded),
        out_specs=(vmem, vmem, vmem),
        scratch_shapes=held
        + [
            dma((len(loaded),)),
            pltpu.VMEM((sectors // per_chunk, 8, chunk), jnp.int32),
            pltpu.VMEM(own_shape, bf16),
            pltpu.VMEM(bins_shape, f32),
            pltpu.VMEM((rows, 1), f32),
            pltpu.VMEM((tile, chunk), f32),
            pltpu.VMEM(bins_shape, f32),
            pltpu.VMEM((count, *bins_shape), f32),
            pltpu.VMEM(own_shape, f32),
            pltpu.VMEM(pieces, f32),
            pltpu.VMEM((2, reps, rows, 2 * width), f32),
            pltpu.VMEM((2 * rows, 2 * width), f32),
            pltpu.VMEM((2, rows, width), f32),
            pltpu.VMEM(pieces, f32),
            pltpu.VMEM(pieces, f32),
            pltpu.VMEM((3, *images.shape), f32),
            pltpu.VMEM(edge, f32),
            pltpu.VMEM(images.shape, f32),
            pltpu.VMEM(edge, f32),
            pltpu.VMEM(images.shape, f32),
            dma((4,)),
            dma((4,)),
            dma((views,)),
            dma((views,)),
            dma((count,)),
            dma((count,)),
            dma((4 * reps,)),
            dma((4 * reps,)),
            dma((views,)),
            dma((views,)),
        ],
        compiler_params=pltpu.CompilerParams(
            collective_id=0, has_side_effects=True, vmem_limit_bytes=60 * 1024 * 1024
        ),
    )(*staged, *loaded)


def on_device(
    images,
    scaled_duals,
    proj_tiles,
    tile_ids,
    pixel_blocks,
    tof_offsets,
    counts,
    sinogram,
    coil_maps,
    kspace,
    sampling,
):
    rep_count = lax.axis_size("rep")
    view_count = lax.axis_size("view")
    slab_count = lax.axis_size("slab")
    row_block = images.shape[2]
    width = images.shape[3]
    groups = coil_maps.shape[3]

    own_images = images[:, 0]

    grid = np.arange(width)
    angle = (np.outer(grid, grid) % width) * (2.0 * np.pi / width)
    cosine, sine = np.cos(angle) / np.sqrt(width), np.sin(angle) / np.sqrt(width)
    by_rep = grid.reshape(groups, rep_count, row_block).transpose(1, 0, 2).reshape(rep_count, -1)
    row_tables = []
    for rep in range(rep_count):
        seen = np.concatenate([by_rep[(rep - step) % rep_count] for step in range(rep_count)])
        row_tables.append(
            np.concatenate([table[by_rep[rep]][:, seen] for table in (cosine, sine)], axis=0)
        )
    tables = [jnp.asarray(part) for part in split_table(np.concatenate([cosine, sine], axis=1))]
    tables += [jnp.asarray(part) for part in split_table(np.stack(row_tables))]
    rows = groups * row_block
    updated, shrunk, dual_next = step_call(
        (view_count, rep_count, slab_count),
        (
            counts,
            tile_ids,
            pixel_blocks,
            tof_offsets,
            sinogram,
            own_images,
            sampling.reshape(groups, row_block),
        ),
        (
            proj_tiles,
            scaled_duals[:, 0],
            coil_maps.reshape(2, rows, width),
            kspace.reshape(2, rows, width),
            *tables,
        ),
    )
    return (updated[:, None], shrunk[:, None], dual_next[:, None])


def solution(mesh):
    placed = (
        P(None, ("grp", "slab"), ("view", "rep"), None),
        P(None, ("grp", "slab"), ("view", "rep"), None),
        P(),
        P(),
        P(),
        P(),
        P(),
        P(("grp", "slab"), None),
        P(None, "view", ("grp", "slab"), None, "rep", None, None),
        P(None, "view", ("grp", "slab"), None, "rep", None, None),
        P(("grp", "slab"), None, "rep", None),
    )
    return jax.shard_map(
        on_device,
        mesh=mesh,
        in_specs=placed,
        out_specs=(
            P(None, ("grp", "slab"), ("view", "rep"), None),
            P(None, ("grp", "slab"), ("view", "rep"), None),
            P(None, ("grp", "slab"), ("view", "rep"), None),
        ),
        check_vma=False,
    )
```
